32 devices in a mesh: seq: 4 (over y, x), fsdp: 8 (over z, core).
Axes of the slice: x: 2, y: 2, z: 4, core: 2. Of those that a mesh axis runs over, the one named last changes fastest.
Arguments:
- patches: bfloat16 [8, 1024, 1152], P('fsdp'), may hold values from -6 to 6
- counts: int32 [8, 4], P('fsdp'), may hold values from 1 to 253, as said below
- starts: int32 [8, 4], P('fsdp'), may hold values from 0 to 511, as said below
- embeds: bfloat16 [8, 512, 2048], P('fsdp', 'seq'), may hold values from -6 to 6
- route_ids: int32 [8, 512, 6], P('fsdp'), may hold values from 0 to 63, all different within a row; in each aligned block of 512 rows (0 to 511, 512 to 1023, ..., all dimensions but the last counted through in order) at most 64 rows name the same one
- route_weights: float32 [8, 512, 6], P('fsdp'), may hold values from 0.1 to 0.6
- vit_gain: float32 [1152], replicated, may hold values from 0.5 to 1.5
- vit_fc1: bfloat16 [1152, 4304], P('fsdp', 'seq'), may hold values from -0.1875 to 0.1875
- vit_fc2: bfloat16 [1152, 4304], P('fsdp', 'seq'), may hold values from -0.09375 to 0.09375
- proj_gain: float32 [4608], replicated, may hold values from 0.5 to 1.5
- proj_weight: bfloat16 [4608, 2048], P('fsdp', 'seq'), may hold values from -0.09375 to 0.09375
- moe_gain: float32 [2048], replicated, may hold values from 0.5 to 1.5
- shared_gate: bfloat16 [2048, 2816], P('fsdp', 'seq'), may hold values from -0.125 to 0.125
- shared_up: bfloat16 [2048, 2816], P('fsdp', 'seq'), may hold values from -0.125 to 0.125
- shared_down: bfloat16 [2048, 2816], P('fsdp', 'seq'), may hold values from -0.109375 to 0.109375
- expert_gate: bfloat16 [2048, 4, 1408], P('fsdp', 'seq'), may hold values from -0.125 to 0.125
- expert_up: bfloat16 [2048, 4, 1408], P('fsdp', 'seq'), may hold values from -0.125 to 0.125
- expert_down: bfloat16 [2048, 4, 1408], P('fsdp', 'seq'), may hold values from -0.15625 to 0.15625
Outputs:
- layer_out: bfloat16 [8, 512, 2048], P('fsdp', 'seq')
The draws below stay inside these ranges and needn't reach their ends.
Inputs may be any that keep to these rules, and one draw needn't show every extreme that they name: Per stream the counts of its 4 images sum to 256. `starts`: images of a stream lie in order in disjoint runs of positions inside its 512 positions; in each stream the 128 positions of some one index of seq are all visual. `route_ids`: the 6 experts of a token differ; in each stream no expert is chosen by more than 64 tokens.
All inputs are finite; a program needn't handle non-finite values.
Results may differ from the reference program's by a relative error of at most 0.014.
Values may be sent and summed in bfloat16 or wider, within the bound.
A program may use at most 128 MiB of HBM per device.

```python
import math
import jax
import jax.numpy as jnp
import numpy as np
from jax import lax

VIT = 1152
VIT_FF = 4304
D = 2048
HID = 1408
EXPERTS = 64
TOP = 6
TOK_DEV = 128
EXP_SEQ = 1
PROJ_IN = 4608
SH_HID = 2816
WIN = 4
GROUPS = 8
SEQ_LEN = 512
VTOK = 256
PATCHES = 1024
IMAGES = 4
ROUTE_CAP = 64
N_SEQ = 4


def image_layout(key):

    def one_stream(subkey, is_first):
        key_cut, key_owner, key_before, key_spread = jax.random.split(subkey, 4)
        random_cuts = jnp.sort(jax.random.permutation(key_cut, VTOK - 1)[:IMAGES - 1] + 1).astype(jnp.int32)
        fixed_cuts = jnp.arange(1, IMAGES, dtype=jnp.int32)
        cuts = jnp.where(is_first, fixed_cuts, random_cuts).astype(jnp.int32)
        bounds = jnp.concatenate([jnp.zeros((1,), jnp.int32), cuts, jnp.full((1,), VTOK, jnp.int32)])
        counts = (bounds[1:] - bounds[:-1]).astype(jnp.int32)
        begins = bounds[:-1]
        end_index = bounds[1:]
        owner_block = jax.random.randint(key_owner, (), 0, SEQ_LEN // TOK_DEV)
        text_slots = SEQ_LEN - VTOK
        lower_lead = jnp.maximum(0, owner_block * TOK_DEV - VTOK + TOK_DEV)
        upper_lead = jnp.minimum(text_slots, owner_block * TOK_DEV)
        before = lower_lead + jax.random.randint(key_before, (), 0, 1 << 20) % (upper_lead - lower_lead + 1)
        first_vis = owner_block * TOK_DEV - before
        spread = jnp.sort(jax.random.randint(key_spread, (IMAGES,), 0, text_slots + 1))
        covers = (end_index > first_vis) & (begins < first_vis + TOK_DEV)
        earlier = end_index <= first_vis
        text_before = jnp.where(covers, before, jnp.where(earlier, jnp.minimum(spread, before), jnp.maximum(spread, before)))
        starts = (begins + text_before).astype(jnp.int32)
        return (counts, starts)
    stream_keys = jax.random.split(jax.random.fold_in(key, 11), GROUPS)
    first_flags = jnp.arange(GROUPS, dtype=jnp.int32) == 0
    return jax.vmap(one_stream)(stream_keys, first_flags)


def draw_counts(key, part):
    return image_layout(key)[0]


def draw_starts(key, part):
    return image_layout(key)[1]


def block_levels(stream_key, extent, shards, low, high):
    factor_of = 1.0
    for dim, shards_of in shards:
        steps = jax.random.uniform(jax.random.fold_in(jax.random.fold_in(stream_key, 6), dim), (shards_of,), jnp.float32, low / len(shards), high / len(shards))
        factor_of = factor_of * jnp.repeat(jnp.exp(steps), extent[dim] // shards_of).reshape((-1,) + (1,) * (len(extent) - 1 - dim))
    return factor_of


def assign_block(stream_key, own, number, rows, number_of, top, most, lean):
    sequence = jax.random.permutation(stream_key, number_of)
    heavy_load, usual = shares(number_of, rows * top, most, lean, True), shares(number_of, rows * top, most, lean, False)
    places = jnp.arange(number_of)

    def named(sizes, offset_by):
        used = int((sizes > 0).sum())
        fixed = max(1, used // 4)
        passed = fixed + (places - fixed + offset_by * (used - fixed)) % max(1, number_of - fixed)
        return jnp.zeros((number_of,), jnp.int32).at[sequence[jnp.where(places < fixed, places, passed)]].set(jnp.asarray(sizes, jnp.int32))

    sizes = jnp.where(number % 4 == 0, named(heavy_load, number // 4), named(usual, number - number // 4 - 1))
    mixed = jax.random.permutation(jax.random.fold_in(own, 3), number_of)
    giver, sink = mixed[0:number_of // 2 * 2:2], mixed[1:number_of // 2 * 2:2]
    slack = jnp.minimum(sizes[giver] - 1, most - sizes[sink]) // 2
    slack = jnp.where((giver == sequence[0]) | (sink == sequence[0]) | (sizes[sink] == 0), 0, jnp.maximum(slack, 0))
    passed = jax.random.randint(jax.random.fold_in(own, 4), (number_of // 2,), 0, 1 << 20) % (slack + 1)
    sizes = sizes.at[giver].add(-passed).at[sink].add(passed)
    items = jnp.searchsorted(jnp.cumsum(sizes), jnp.arange(rows * top), side="right").astype(jnp.int32)
    listing = items.reshape(top, rows).T
    listing = listing[jax.random.permutation(jax.random.fold_in(own, 1), rows)]
    offset_by = jax.random.randint(jax.random.fold_in(own, 2), (rows, 1), 0, top)
    return jnp.take_along_axis(listing, (jnp.arange(top)[None, :] + offset_by) % top, axis=1)


def shares(number_of, total, reach, slope, full):
    loads = [(1 << 20) // math.isqrt(rank ** slope) + 1 for rank in range(1, number_of + 1)]
    largest = reach if full else min(reach, max(-(-total // number_of), total * loads[0] // sum(loads)))
    least = 1 if total - largest >= number_of - 1 else 0
    given, spare = [largest] + [least] * (number_of - 1), total - largest - least * (number_of - 1)
    while spare > 0:
        movable = [i for i in range(1, number_of) if given[i] < largest] or [i for i in range(1, number_of) if given[i] < reach]
        whole, budget = sum([loads[i] for i in movable]), spare
        for i in movable:
            addition = min(reach - given[i], max(1, budget * loads[i] // whole), spare)
            given[i] = given[i] + addition
            spare = spare - addition
    return np.array(given)


def scatter_about(key, extent, scale, reach, pieces=(), kind=jnp.bfloat16):
    entries = jax.random.normal(key, extent, jnp.float32) * scale
    if len(pieces) > 0:
        entries = block_levels(key, extent, pieces, -0.22, 0.18) * entries
    return jnp.clip(entries, min=-reach, max=reach).astype(kind)


def setup_inputs(seed: int = 0) -> dict:
    splits = jax.random.split(jax.random.key(seed), 19)
    patches = scatter_about(splits[0], (GROUPS, PATCHES, VIT), 1.0, 6.0, ((0, 8),))
    counts = draw_counts(jax.random.fold_in(splits[18], 71), 0)
    starts = draw_starts(jax.random.fold_in(splits[18], 71), 0)
    embeds = scatter_about(splits[3], (GROUPS, SEQ_LEN, D), 1.0, 6.0, ((0, 8), (1, 4)))
    route_ids_keys = jax.random.split(jax.random.fold_in(splits[4], 1), GROUPS * SEQ_LEN // SEQ_LEN)
    route_ids_turns = jax.random.permutation(jax.random.fold_in(splits[4], 3), GROUPS * SEQ_LEN // SEQ_LEN)
    route_ids = jax.vmap(lambda own, number: assign_block(jax.random.fold_in(splits[4], 2), own, number, SEQ_LEN, EXPERTS, TOP, ROUTE_CAP, 2))(route_ids_keys, route_ids_turns).reshape((GROUPS, SEQ_LEN, TOP))
    route_weights = jnp.clip(0.1 + 0.5 * jax.random.uniform(splits[5], (GROUPS, SEQ_LEN, TOP), jnp.float32) ** block_levels(splits[5], (GROUPS, SEQ_LEN, TOP), ((0, 8),), -0.2, 0.2), 0.1, 0.6)
    vit_gain = jnp.clip(1.0 + 0.1 * jax.random.normal(splits[6], (VIT,), jnp.float32), 0.5, 1.5)
    vit_fc1 = scatter_about(splits[7], (VIT, VIT_FF), VIT ** -0.5, 0.1875, ((0, 8), (1, 4)))
    vit_fc2 = scatter_about(splits[8], (VIT, VIT_FF), VIT_FF ** -0.5, 0.09375, ((0, 8), (1, 4)))
    proj_gain = jnp.clip(1.0 + 0.1 * jax.random.normal(splits[9], (PROJ_IN,), jnp.float32), 0.5, 1.5)
    proj_weight = scatter_about(splits[10], (PROJ_IN, D), PROJ_IN ** -0.5, 0.09375, ((0, 8), (1, 4)))
    moe_gain = jnp.clip(1.0 + 0.1 * jax.random.normal(splits[11], (D,), jnp.float32), 0.5, 1.5)
    shared_gate = scatter_about(splits[12], (D, SH_HID), D ** -0.5, 0.125, ((0, 8), (1, 4)))
    shared_up = scatter_about(splits[13], (D, SH_HID), D ** -0.5, 0.125, ((0, 8), (1, 4)))
    shared_down = scatter_about(splits[14], (D, SH_HID), SH_HID ** -0.5, 0.109375, ((0, 8), (1, 4)))
    expert_gate = scatter_about(splits[15], (D, WIN, HID), D ** -0.5, 0.125, ((0, 8), (1, 4)))
    expert_up = scatter_about(splits[16], (D, WIN, HID), D ** -0.5, 0.125, ((0, 8), (1, 4)))
    expert_down = scatter_about(splits[17], (D, WIN, HID), HID ** -0.5, 0.15625, ((0, 8), (1, 4)))
    return dict(patches=patches, counts=counts, starts=starts, embeds=embeds, route_ids=route_ids, route_weights=route_weights, vit_gain=vit_gain, vit_fc1=vit_fc1, vit_fc2=vit_fc2, proj_gain=proj_gain, proj_weight=proj_weight, moe_gain=moe_gain, shared_gate=shared_gate, shared_up=shared_up, shared_down=shared_down, expert_gate=expert_gate, expert_up=expert_up, expert_down=expert_down)


ln_epsilon = 1e-05
rms_epsilon = 1e-06

def layer_norm(values, gain_vec):
    center = values - lax.optimization_barrier(jnp.mean(values, axis=-1, keepdims=True))
    spread = lax.optimization_barrier(jnp.mean(center * center, axis=-1, keepdims=True))
    return center * lax.rsqrt(spread + ln_epsilon) * gain_vec

def rms_norm(values, gain_vec):
    square = lax.optimization_barrier(jnp.mean(values * values, axis=-1, keepdims=True))
    return values * lax.rsqrt(square + rms_epsilon) * gain_vec

def visual_positions(counts, starts, total):
    end_index = jnp.cumsum(counts).astype(jnp.int32)
    begins = (end_index - counts).astype(jnp.int32)
    token_index = jnp.arange(total, dtype=jnp.int32)
    inside = (token_index[:, None] >= begins[None, :]) & (token_index[:, None] < end_index[None, :])
    placed = starts[None, :] + token_index[:, None] - begins[None, :]
    return lax.optimization_barrier(jnp.sum(jnp.where(inside, placed, 0), axis=1)).astype(jnp.int32)

def routed_rows(gathered, route_ids, route_weights, expert, capacity, gate_w, up_w, down_w):
    hit_mask = route_ids == expert
    chosen = jnp.any(hit_mask, axis=1)
    weight_sum = lax.optimization_barrier(jnp.sum(jnp.where(hit_mask, route_weights, 0.0), axis=1))
    count_rows = gathered.shape[0]
    slot_rank = (jnp.cumsum(chosen.astype(jnp.int32)) - 1).astype(jnp.int32)
    target = jnp.where(chosen, slot_rank, capacity).astype(jnp.int32)
    slot_rows = jnp.zeros((capacity,), jnp.int32).at[target].set(jnp.arange(count_rows, dtype=jnp.int32), mode='drop')
    is_live = jnp.arange(capacity, dtype=jnp.int32) < jnp.sum(chosen.astype(jnp.int32)).astype(jnp.int32)
    picked = jnp.take(gathered, slot_rows, axis=0)
    gate_part = jnp.dot(picked, gate_w, preferred_element_type=jnp.float32)
    up_part = jnp.dot(picked, up_w, preferred_element_type=jnp.float32)
    hidden = (jax.nn.silu(gate_part) * up_part).astype(jnp.bfloat16)
    result = lax.dot_general(hidden, down_w, (((1,), (1,)), ((), ())), preferred_element_type=jnp.float32)
    factor = jnp.where(is_live, jnp.take(weight_sum, slot_rows), 0.0)
    return (slot_rows, result * factor[:, None])

def one_stream(patches, counts, starts, embeds, route_ids, route_weights, vit_gain, vit_fc1, vit_fc2, proj_gain, proj_weight, moe_gain, shared_gate, shared_up, shared_down, expert_gate, expert_up, expert_down):
    image_rows = patches.astype(jnp.float32)
    normed = layer_norm(image_rows, vit_gain).astype(jnp.bfloat16)
    hidden = jax.nn.gelu(jnp.dot(normed, vit_fc1, preferred_element_type=jnp.float32), approximate=True).astype(jnp.bfloat16)
    block_width = VIT_FF // N_SEQ
    mixed_sum = jnp.zeros(image_rows.shape, jnp.float32)
    for block_index in range(N_SEQ):
        col_start = block_index * block_width
        product = lax.dot_general(hidden[:, col_start:col_start + block_width], vit_fc2[:, col_start:col_start + block_width], (((1,), (1,)), ((), ())), preferred_element_type=jnp.float32)
        rounded = lax.optimization_barrier(product.astype(jnp.bfloat16))
        mixed_sum = mixed_sum + rounded.astype(jnp.float32)
    residual = image_rows + mixed_sum
    proj_in = layer_norm(residual.reshape(-1, PROJ_IN), proj_gain).astype(jnp.bfloat16)
    visual = jnp.dot(proj_in, proj_weight, preferred_element_type=jnp.float32).astype(jnp.bfloat16)
    positions = visual_positions(counts, starts, VTOK)
    merged = embeds.at[positions].set(visual, mode='drop')
    normed_tokens = rms_norm(merged.astype(jnp.float32), moe_gain).astype(jnp.bfloat16)
    shared_width = SH_HID // N_SEQ
    capacity = SEQ_LEN // 8
    running = jnp.zeros(merged.shape, jnp.float32)
    for block_index in range(N_SEQ):
        col_start = block_index * shared_width
        gate_part = jnp.dot(normed_tokens, shared_gate[:, col_start:col_start + shared_width], preferred_element_type=jnp.float32)
        up_part = jnp.dot(normed_tokens, shared_up[:, col_start:col_start + shared_width], preferred_element_type=jnp.float32)
        shared_hidden = (jax.nn.silu(gate_part) * up_part).astype(jnp.bfloat16)
        partial_value = lax.dot_general(shared_hidden, shared_down[:, col_start:col_start + shared_width], (((1,), (1,)), ((), ())), preferred_element_type=jnp.float32)
        for local_expert in range(EXP_SEQ):
            expert = block_index * EXP_SEQ + local_expert
            slot_rows, values = routed_rows(normed_tokens, route_ids, route_weights, expert, capacity, expert_gate[:, expert, :], expert_up[:, expert, :], expert_down[:, expert, :])
            partial_value = partial_value.at[slot_rows].add(values)
        rounded = lax.optimization_barrier(partial_value.astype(jnp.bfloat16))
        running = running + rounded.astype(jnp.float32)
    return (merged.astype(jnp.float32) + running).astype(jnp.bfloat16)

def reference(patches, counts, starts, embeds, route_ids, route_weights, vit_gain, vit_fc1, vit_fc2, proj_gain, proj_weight, moe_gain, shared_gate, shared_up, shared_down, expert_gate, expert_up, expert_down):
    streams = []
    for stream in range(GROUPS):
        streams.append(one_stream(patches[stream], counts[stream], starts[stream], embeds[stream], route_ids[stream], route_weights[stream], vit_gain, vit_fc1, vit_fc2, proj_gain, proj_weight, moe_gain, shared_gate, shared_up, shared_down, expert_gate, expert_up, expert_down))
    return jnp.stack(streams)
```

```python
import jax
import jax.numpy as jnp
from jax import lax
from jax.sharding import PartitionSpec as P

ln_epsilon = 1e-05
rms_epsilon = 1e-06
bf16 = jnp.bfloat16
f32 = jnp.float32


def layer_norm(values, gain_vec):
    center = values - jnp.mean(values, axis=-1, keepdims=True)
    spread = jnp.mean(center * center, axis=-1, keepdims=True)
    return center * lax.rsqrt(spread + ln_epsilon) * gain_vec


def rms_norm(values, gain_vec):
    square = jnp.mean(values * values, axis=-1, keepdims=True)
    return values * lax.rsqrt(square + rms_epsilon) * gain_vec


def visual_positions(counts, starts, total):
    images = jnp.arange(counts.shape[0], dtype=jnp.int32)
    end_index = jnp.sum(jnp.where(images[None, :] <= images[:, None], counts[None, :], 0), axis=1)
    begins = end_index - counts
    token_index = jnp.arange(total, dtype=jnp.int32)
    inside = (token_index[:, None] >= begins[None, :]) & (token_index[:, None] < end_index[None, :])
    placed = starts[None, :] + token_index[:, None] - begins[None, :]
    return jnp.sum(jnp.where(inside, placed, 0), axis=1)


def exchange(blocks, axis):
    return lax.all_to_all(blocks, axis, split_axis=0, concat_axis=0, tiled=True)


def spread_blocks(block, axis, count):
    return exchange(jnp.broadcast_to(block[None], (count,) + block.shape), axis)


def dot_t(left, right):
    return lax.dot_general(left, right, (((1,), (1,)), ((), ())), preferred_element_type=f32)


def dot(left, right):
    return jnp.dot(left, right, preferred_element_type=f32)


def shards(
    patches,
    counts,
    starts,
    embeds,
    route_ids,
    route_weights,
    vit_gain,
    vit_fc1,
    vit_fc2,
    proj_gain,
    proj_weight,
    moe_gain,
    shared_gate,
    shared_up,
    shared_down,
    expert_gate,
    expert_up,
    expert_down,
):
    n_seq = lax.axis_size("seq")
    me = lax.axis_index("seq")
    n_fsdp = lax.axis_size("fsdp")

    vit_first = lax.all_gather(vit_fc1, "fsdp", axis=0, tiled=True)
    vit_fc2, vit_first = lax.optimization_barrier((vit_fc2, vit_first))
    vit_second = lax.all_gather(vit_fc2, "fsdp", axis=0, tiled=True)
    proj_weight, vit_second = lax.optimization_barrier((proj_weight, vit_second))
    projector = lax.all_gather(proj_weight, "fsdp", axis=0, tiled=True)
    shared_gate, projector = lax.optimization_barrier((shared_gate, projector))
    gate_shared = lax.all_gather(shared_gate, "fsdp", axis=0, tiled=True)
    shared_up, gate_shared = lax.optimization_barrier((shared_up, gate_shared))
    up_shared = lax.all_gather(shared_up, "fsdp", axis=0, tiled=True)
    shared_down, up_shared = lax.optimization_barrier((shared_down, up_shared))
    down_shared = lax.all_gather(shared_down, "fsdp", axis=0, tiled=True)

    width = embeds.shape[2]
    tok_dev = embeds.shape[1]
    all_embeds = spread_blocks(embeds[0], "seq", n_seq).reshape(n_seq * tok_dev, width)
    n_tok = n_seq * tok_dev

    rows = patches.shape[1]
    my_rows = rows // n_seq
    normed = layer_norm(patches[0].astype(f32), vit_gain).astype(bf16)
    hidden = jax.nn.gelu(dot(normed, vit_first), approximate=True).astype(bf16)
    product = dot_t(hidden, vit_second).astype(bf16)
    blocks = exchange(product.reshape(n_seq, my_rows, product.shape[1]), "seq")
    mixed = jnp.sum(blocks.astype(f32), axis=0)
    mine = lax.dynamic_slice_in_dim(patches[0], me * my_rows, my_rows, axis=0)
    residual = mine.astype(f32) + mixed

    joined = residual.shape[1] * 4
    proj_part = layer_norm(residual.reshape(-1, joined), proj_gain).astype(bf16)
    proj_in = spread_blocks(proj_part, "seq", n_seq).reshape(-1, joined)
    visual_part = dot(proj_in, projector).astype(bf16)
    n_vis = visual_part.shape[0]
    visual = spread_blocks(visual_part, "seq", n_seq).transpose(1, 0, 2).reshape(n_vis, width)

    positions = visual_positions(counts[0], starts[0], n_vis)
    token_ids = jnp.arange(n_tok, dtype=jnp.int32)
    place = positions[None, :] == token_ids[:, None]
    is_visual = jnp.any(place, axis=1)
    placed_visual = dot(place.astype(bf16), visual).astype(bf16)
    merged = jnp.where(is_visual[:, None], placed_visual, all_embeds)
    tokens = rms_norm(merged.astype(f32), moe_gain).astype(bf16)

    capacity = n_tok // 8
    hit_mask = route_ids[0] == me
    chosen = jnp.any(hit_mask, axis=1)
    weight_sum = jnp.sum(jnp.where(hit_mask, route_weights[0], 0.0), axis=1)
    before = (token_ids[None, :] < token_ids[:, None]) & chosen[None, :]
    rank = jnp.sum(before.astype(f32), axis=1).astype(jnp.int32)
    slot_ids = jnp.arange(capacity, dtype=jnp.int32)
    pick = chosen[None, :] & (rank[None, :] == slot_ids[:, None])
    picked = dot(pick.astype(bf16), tokens).astype(bf16)
    depth = expert_gate.shape[0]
    hid = expert_gate.shape[2]
    picked_cols = exchange(picked.reshape(capacity, n_fsdp, depth).transpose(1, 0, 2), "fsdp")
    picked_cols = picked_cols.reshape(n_fsdp * capacity, depth)
    gate_up = jnp.concatenate(
        [dot(picked_cols, expert_gate[:, 0, :]), dot(picked_cols, expert_up[:, 0, :])], axis=1
    ).astype(bf16)
    sums = jnp.sum(exchange(gate_up.reshape(n_fsdp, capacity, 2 * hid), "fsdp").astype(f32), axis=0)
    expert_hidden = (jax.nn.silu(sums[:, :hid]) * sums[:, hid:]).astype(bf16)
    all_hidden = spread_blocks(expert_hidden, "fsdp", n_fsdp).reshape(n_fsdp * capacity, hid)
    down_cols = dot_t(all_hidden, expert_down[:, 0, :]).astype(bf16)
    values = exchange(down_cols.reshape(n_fsdp, capacity, depth), "fsdp")
    values = values.transpose(1, 0, 2).reshape(capacity, width)
    routed = lax.dot_general(
        pick.astype(bf16), values, (((0,), (0,)), ((), ())), preferred_element_type=f32
    )

    shared_hidden = (jax.nn.silu(dot(tokens, gate_shared)) * dot(tokens, up_shared)).astype(bf16)
    partial_value = (dot_t(shared_hidden, down_shared) + routed * weight_sum[:, None]).astype(bf16)
    terms = exchange(partial_value.reshape(n_seq, tok_dev, width), "seq")
    summed = jnp.sum(terms.astype(f32), axis=0)
    own = lax.dynamic_slice_in_dim(merged, me * tok_dev, tok_dev, axis=0)
    return (own.astype(f32) + summed).astype(bf16)[None]


def solution(mesh):
    placed = (
        P("fsdp", None, None),
        P("fsdp", None),
        P("fsdp", None),
        P("fsdp", "seq", None),
        P("fsdp", None, None),
        P("fsdp", None, None),
        P(),
        P("fsdp", "seq"),
        P("fsdp", "seq"),
        P(),
        P("fsdp", "seq"),
        P(),
        P("fsdp", "seq"),
        P("fsdp", "seq"),
        P("fsdp", "seq"),
        P("fsdp", "seq", None),
        P("fsdp", "seq", None),
        P("fsdp", "seq", None),
    )
    return jax.shard_map(
        shards, mesh=mesh, in_specs=placed, out_specs=P("fsdp", "seq", None), check_vma=False
    )
```

```python
import jax
import jax.numpy as jnp
from jax import lax
from jax.sharding import PartitionSpec as P

ln_epsilon = 1e-05
rms_epsilon = 1e-06
bf16 = jnp.bfloat16
f32 = jnp.float32


def layer_norm(values, gain_vec):
    center = values - jnp.mean(values, axis=-1, keepdims=True)
    spread = jnp.mean(center * center, axis=-1, keepdims=True)
    return center * lax.rsqrt(spread + ln_epsilon) * gain_vec


def rms_norm(values, gain_vec):
    square = jnp.mean(values * values, axis=-1, keepdims=True)
    return values * lax.rsqrt(square + rms_epsilon) * gain_vec


def visual_positions(counts, starts, total):
    images = jnp.arange(counts.shape[0], dtype=jnp.int32)
    end_index = jnp.sum(jnp.where(images[None, :] <= images[:, None], counts[None, :], 0), axis=1)
    begins = end_index - counts
    token_index = jnp.arange(total, dtype=jnp.int32)
    inside = (token_index[:, None] >= begins[None, :]) & (token_index[:, None] < end_index[None, :])
    placed = starts[None, :] + token_index[:, None] - begins[None, :]
    return jnp.sum(jnp.where(inside, placed, 0), axis=1)


def exchange(blocks, axis, groups=None):
    return lax.all_to_all(
        blocks, axis, split_axis=0, concat_axis=0, tiled=True, axis_index_groups=groups
    )


def spread_blocks(block, axis, count, groups=None):
    return exchange(jnp.broadcast_to(block[None], (count,) + block.shape), axis, groups)


def dot_t(left, right):
    return lax.dot_general(left, right, (((1,), (1,)), ((), ())), preferred_element_type=f32)


def dot(left, right):
    return jnp.dot(left, right, preferred_element_type=f32)


def shards(
    patches,
    counts,
    starts,
    embeds,
    route_ids,
    route_weights,
    vit_gain,
    vit_fc1,
    vit_fc2,
    proj_gain,
    proj_weight,
    moe_gain,
    shared_gate,
    shared_up,
    shared_down,
    expert_gate,
    expert_up,
    expert_down,
):
    n_seq = lax.axis_size("seq")
    me = lax.axis_index("seq")
    n_fsdp = lax.axis_size("fsdp")

    half = n_fsdp // 2
    swap = [(i, i ^ 1) for i in range(n_fsdp)]
    lines = [[2 * i + c for i in range(half)] for c in range(2)]

    width = embeds.shape[2]
    tok_dev = embeds.shape[1]
    all_embeds = spread_blocks(embeds[0], "seq", n_seq).reshape(n_seq * tok_dev, width)
    n_tok = n_seq * tok_dev

    vit_both = lax.all_gather(jnp.stack([vit_fc1, vit_fc2]), "fsdp", axis=1, tiled=True)
    proj_weight, vit_both, all_embeds = lax.optimization_barrier(
        (proj_weight, vit_both, all_embeds)
    )
    vit_first, vit_second = vit_both[0], vit_both[1]
    projector = lax.all_gather(proj_weight, "fsdp", axis=0, tiled=True)
    shared = jnp.stack([shared_gate, shared_up, shared_down])

    rows = patches.shape[1]
    my_rows = rows // n_seq
    normed = layer_norm(patches[0].astype(f32), vit_gain).astype(bf16)
    hidden = jax.nn.gelu(dot(normed, vit_first), approximate=True).astype(bf16)
    product = dot_t(hidden, vit_second).astype(bf16)
    blocks = exchange(product.reshape(n_seq, my_rows, product.shape[1]), "seq")
    shared, blocks = lax.optimization_barrier((shared, blocks))
    shared = lax.all_gather(shared, "fsdp", axis=1, tiled=True)
    gate_shared, up_shared, down_shared = shared[0], shared[1], shared[2]
    mixed = jnp.sum(blocks.astype(f32), axis=0)
    mine = lax.dynamic_slice_in_dim(patches[0], me * my_rows, my_rows, axis=0)
    residual = mine.astype(f32) + mixed

    joined = residual.shape[1] * 4
    proj_part = layer_norm(residual.reshape(-1, joined), proj_gain).astype(bf16)
    proj_in = spread_blocks(proj_part, "seq", n_seq).reshape(-1, joined)
    visual_part = dot(proj_in, projector).astype(bf16)
    n_vis = visual_part.shape[0]
    visual = spread_blocks(visual_part, "seq", n_seq).transpose(1, 0, 2).reshape(n_vis, width)

    positions = visual_positions(counts[0], starts[0], n_vis)
    token_ids = jnp.arange(n_tok, dtype=jnp.int32)
    place = positions[None, :] == token_ids[:, None]
    is_visual = jnp.any(place, axis=1)
    placed_visual = dot(place.astype(bf16), visual).astype(bf16)
    merged = jnp.where(is_visual[:, None], placed_visual, all_embeds)
    tokens = rms_norm(merged.astype(f32), moe_gain).astype(bf16)

    shared_hidden = (jax.nn.silu(dot(tokens, gate_shared)) * dot(tokens, up_shared)).astype(bf16)
    shared_value = dot_t(shared_hidden, down_shared).astype(bf16)
    terms = exchange(shared_value.reshape(n_seq, tok_dev, width), "seq")

    capacity = n_tok // 8
    experts = jnp.arange(n_seq, dtype=jnp.int32)
    hit_mask = route_ids[0][None] == experts[:, None, None]
    chosen = jnp.any(hit_mask, axis=2)
    weight_sum = jnp.sum(jnp.where(hit_mask, route_weights[0][None], 0.0), axis=2)
    earlier = (token_ids[:, None] < token_ids[None, :]).astype(bf16)
    rank = dot(chosen.astype(bf16), earlier).astype(jnp.int32)
    rank = jnp.where(chosen, rank, -1)
    slot_ids = jnp.arange(capacity, dtype=jnp.int32)
    my_rank = lax.dynamic_index_in_dim(rank, me, 0, keepdims=False)
    pick = my_rank[None, :] == slot_ids[:, None]

    picked = dot(pick.astype(bf16), tokens).astype(bf16)
    depth = expert_gate.shape[0]
    hid = expert_gate.shape[2]
    core = lax.axis_index("fsdp") % 2
    picked_cols = exchange(picked.reshape(capacity, n_fsdp, depth).transpose(1, 0, 2), "fsdp")
    picked_cols = picked_cols.reshape(half, 2, capacity, depth).transpose(1, 0, 2, 3)
    picked_cols = picked_cols.reshape(n_fsdp * capacity, depth)
    gate_up = jnp.concatenate(
        [dot(picked_cols, expert_gate[:, 0, :]), dot(picked_cols, expert_up[:, 0, :])], axis=1
    ).astype(bf16)
    gate_up = gate_up.reshape(2, half * capacity, 2 * hid)
    keep = lax.dynamic_index_in_dim(gate_up, core, 0, keepdims=False)
    sent = lax.dynamic_index_in_dim(gate_up, 1 - core, 0, keepdims=False)
    sent = lax.ppermute(sent, "fsdp", swap)
    gate_up = (keep.astype(f32) + sent.astype(f32)).astype(bf16)
    gate_up = exchange(gate_up.reshape(half, capacity, 2 * hid), "fsdp", lines)
    sums = jnp.sum(gate_up.astype(f32), axis=0)
    expert_hidden = (jax.nn.silu(sums[:, :hid]) * sums[:, hid:]).astype(bf16)
    line_hidden = spread_blocks(expert_hidden, "fsdp", half, lines)
    other_hidden = lax.ppermute(line_hidden, "fsdp", swap)
    all_hidden = jnp.stack(
        [
            jnp.where(core == 0, line_hidden, other_hidden),
            jnp.where(core == 0, other_hidden, line_hidden),
        ]
    ).reshape(n_fsdp * capacity, hid)
    down_cols = dot_t(all_hidden, expert_down[:, 0, :]).astype(bf16)
    down_cols = down_cols.reshape(2, half, capacity, depth).transpose(1, 0, 2, 3)
    values = exchange(down_cols.reshape(n_fsdp, capacity, depth), "fsdp")
    values = values.transpose(1, 0, 2).reshape(capacity, width)

    all_values = spread_blocks(values, "seq", n_seq)
    own_rank = lax.dynamic_slice_in_dim(rank, me * tok_dev, tok_dev, axis=1)
    own_weight = lax.dynamic_slice_in_dim(weight_sum, me * tok_dev, tok_dev, axis=1)
    total = jnp.sum(terms.astype(f32), axis=0)
    for e in range(n_seq):
        back = own_rank[e][:, None] == slot_ids[None, :]
        total = total + dot(back.astype(bf16), all_values[e]) * own_weight[e][:, None]
    own = lax.dynamic_slice_in_dim(merged, me * tok_dev, tok_dev, axis=0)
    return (own.astype(f32) + total).astype(bf16)[None]


def solution(mesh):
    placed = (
        P("fsdp", None, None),
        P("fsdp", None),
        P("fsdp", None),
        P("fsdp", "seq", None),
        P("fsdp", None, None),
        P("fsdp", None, None),
        P(),
        P("fsdp", "seq"),
        P("fsdp", "seq"),
        P(),
        P("fsdp", "seq"),
        P(),
        P("fsdp", "seq"),
        P("fsdp", "seq"),
        P("fsdp", "seq"),
        P("fsdp", "seq", None),
        P("fsdp", "seq", None),
        P("fsdp", "seq", None),
    )
    return jax.shard_map(
        shards, mesh=mesh, in_specs=placed, out_specs=P("fsdp", "seq", None), check_vma=False
    )
```

```python
import functools

import jax
import jax.numpy as jnp
from jax import lax
from jax.sharding import PartitionSpec as P

ln_epsilon = 1e-05
rms_epsilon = 1e-06
bf16 = jnp.bfloat16
f32 = jnp.float32


def layer_norm(values, gain_vec):
    center = values - jnp.mean(values, axis=-1, keepdims=True)
    spread = jnp.mean(center * center, axis=-1, keepdims=True)
    return center * lax.rsqrt(spread + ln_epsilon) * gain_vec


def rms_norm(values, gain_vec):
    square = jnp.mean(values * values, axis=-1, keepdims=True)
    return values * lax.rsqrt(square + rms_epsilon) * gain_vec


def visual_positions(counts, starts, total):
    images = jnp.arange(counts.shape[0], dtype=jnp.int32)
    end_index = jnp.sum(jnp.where(images[None, :] <= images[:, None], counts[None, :], 0), axis=1)
    begins = end_index - counts
    token_index = jnp.arange(total, dtype=jnp.int32)
    inside = (token_index[:, None] >= begins[None, :]) & (token_index[:, None] < end_index[None, :])
    placed = starts[None, :] + token_index[:, None] - begins[None, :]
    return jnp.sum(jnp.where(inside, placed, 0), axis=1)


def exchange(blocks, axis):
    return lax.all_to_all(blocks, axis, split_axis=0, concat_axis=0, tiled=True)


def spread_blocks(block, axis, count):
    return exchange(jnp.broadcast_to(block[None], (count,) + block.shape), axis)


def dot_t(left, right):
    return lax.dot_general(left, right, (((1,), (1,)), ((), ())), preferred_element_type=f32)


def dot(left, right):
    return jnp.dot(left, right, preferred_element_type=f32)


def shards(
    patches,
    counts,
    starts,
    embeds,
    route_ids,
    route_weights,
    vit_gain,
    vit_fc1,
    vit_fc2,
    proj_gain,
    proj_weight,
    moe_gain,
    shared_gate,
    shared_up,
    shared_down,
    expert_gate,
    expert_up,
    expert_down,
):
    n_seq = lax.axis_size("seq")
    me = lax.axis_index("seq")
    n_fsdp = lax.axis_size("fsdp")

    half = n_fsdp // 2
    swap = [(i, i ^ 1) for i in range(n_fsdp)]
    shifts = [[(i, (i + 2 * k) % n_fsdp) for i in range(n_fsdp)] for k in range(half)]

    width = embeds.shape[2]
    tok_dev = embeds.shape[1]
    all_embeds = spread_blocks(embeds[0], "seq", n_seq).reshape(n_seq * tok_dev, width)
    n_tok = n_seq * tok_dev

    vit_both = lax.all_gather(jnp.stack([vit_fc1, vit_fc2]), "fsdp", axis=1, tiled=True)
    proj_weight, vit_both, all_embeds = lax.optimization_barrier(
        (proj_weight, vit_both, all_embeds)
    )
    vit_first, vit_second = vit_both[0], vit_both[1]
    projector = lax.all_gather(proj_weight, "fsdp", axis=0, tiled=True)
    shared = jnp.stack([shared_gate, shared_up, shared_down])

    rows = patches.shape[1]
    my_rows = rows // n_seq
    normed = layer_norm(patches[0].astype(f32), vit_gain).astype(bf16)
    hidden = jax.nn.gelu(dot(normed, vit_first), approximate=True).astype(bf16)
    product = dot_t(hidden, vit_second).astype(bf16)
    blocks = exchange(product.reshape(n_seq, my_rows, product.shape[1]), "seq")
    shared, blocks = lax.optimization_barrier((shared, blocks))
    shared = lax.all_gather(shared, "fsdp", axis=1, tiled=True)
    gate_shared, up_shared, down_shared = shared[0], shared[1], shared[2]
    mixed = jnp.sum(blocks.astype(f32), axis=0)
    mine = lax.dynamic_slice_in_dim(patches[0], me * my_rows, my_rows, axis=0)
    residual = mine.astype(f32) + mixed

    joined = residual.shape[1] * 4
    proj_part = layer_norm(residual.reshape(-1, joined), proj_gain).astype(bf16)
    proj_in = spread_blocks(proj_part, "seq", n_seq).reshape(-1, joined)
    visual_part = dot(proj_in, projector).astype(bf16)
    n_vis = visual_part.shape[0]
    visual = spread_blocks(visual_part, "seq", n_seq).transpose(1, 0, 2).reshape(n_vis, width)

    positions = visual_positions(counts[0], starts[0], n_vis)
    token_ids = jnp.arange(n_tok, dtype=jnp.int32)
    place = positions[None, :] == token_ids[:, None]
    is_visual = jnp.any(place, axis=1)
    placed_visual = dot(place.astype(bf16), visual).astype(bf16)
    merged = jnp.where(is_visual[:, None], placed_visual, all_embeds)
    tokens = rms_norm(merged.astype(f32), moe_gain).astype(bf16)

    shared_hidden = (jax.nn.silu(dot(tokens, gate_shared)) * dot(tokens, up_shared)).astype(bf16)
    shared_value = dot_t(shared_hidden, down_shared).astype(bf16)

    capacity = n_tok // 8
    experts = jnp.arange(n_seq, dtype=jnp.int32)
    hit_mask = route_ids[0][None] == experts[:, None, None]
    chosen = jnp.any(hit_mask, axis=2)
    weight_sum = jnp.sum(jnp.where(hit_mask, route_weights[0][None], 0.0), axis=2)
    earlier = (token_ids[:, None] < token_ids[None, :]).astype(bf16)
    rank = dot(chosen.astype(bf16), earlier).astype(jnp.int32)
    rank = jnp.where(chosen, rank, -1)
    slot_ids = jnp.arange(capacity, dtype=jnp.int32)
    my_rank = lax.dynamic_index_in_dim(rank, me, 0, keepdims=False)
    pick = my_rank[None, :] == slot_ids[:, None]

    picked = dot(pick.astype(bf16), tokens).astype(bf16)
    depth = expert_gate.shape[0]
    hid = expert_gate.shape[2]
    core = lax.axis_index("fsdp") % 2
    picked_cols = exchange(picked.reshape(capacity, n_fsdp, depth).transpose(1, 0, 2), "fsdp")
    picked_cols = picked_cols.reshape(half, 2, capacity, depth).transpose(1, 0, 2, 3)
    picked_cols = picked_cols.reshape(n_fsdp * capacity, depth)
    gate_up = jnp.concatenate(
        [dot(picked_cols, expert_gate[:, 0, :]), dot(picked_cols, expert_up[:, 0, :])], axis=1
    ).astype(bf16)
    gate_up = gate_up.reshape(2, half * capacity, 2 * hid)
    keep = lax.dynamic_index_in_dim(gate_up, core, 0, keepdims=False)
    sent = lax.dynamic_index_in_dim(gate_up, 1 - core, 0, keepdims=False)
    sent = lax.ppermute(sent, "fsdp", swap)
    gate_up = (keep.astype(f32) + sent.astype(f32)).astype(bf16)
    gate_up = gate_up.reshape(half, capacity, 2 * hid)
    here = lax.axis_index("fsdp") // 2
    gate_up = jnp.concatenate([gate_up, gate_up], axis=0)
    gate_up = lax.dynamic_slice_in_dim(gate_up, here, half, axis=0)
    arrived = [gate_up[0]] + [lax.ppermute(gate_up[k], "fsdp", shifts[k]) for k in range(1, half)]
    shared_value, arrived = lax.optimization_barrier((shared_value, arrived))
    terms = exchange(shared_value.reshape(n_seq, tok_dev, width), "seq")
    sums = functools.reduce(jnp.add, [part.astype(f32) for part in arrived])
    expert_hidden = (jax.nn.silu(sums[:, :hid]) * sums[:, hid:]).astype(bf16)
    line_hidden = [expert_hidden]
    line_hidden += [lax.ppermute(expert_hidden, "fsdp", shifts[k]) for k in range(1, half)]
    other_hidden = [lax.ppermute(part, "fsdp", swap) for part in line_hidden]
    terms, other_hidden = lax.optimization_barrier((terms, other_hidden))
    all_hidden = jnp.concatenate(line_hidden[::-1] + other_hidden[::-1], axis=0)
    down_cols = dot_t(all_hidden, expert_down[:, 0, :]).astype(bf16)
    down_cols = down_cols.reshape(2, half, capacity, depth)
    down_cols = jnp.concatenate([down_cols, down_cols], axis=1)
    down_cols = lax.dynamic_slice_in_dim(down_cols, half - 1 - here, half, axis=1)
    down_cols = jnp.concatenate([down_cols, down_cols], axis=0)
    down_cols = lax.dynamic_slice_in_dim(down_cols, core, 2, axis=0).transpose(1, 0, 2, 3)
    values = exchange(down_cols.reshape(n_fsdp, capacity, depth), "fsdp")
    values = values.transpose(1, 0, 2).reshape(capacity, width)

    all_values = spread_blocks(values, "seq", n_seq)
    own_rank = lax.dynamic_slice_in_dim(rank, me * tok_dev, tok_dev, axis=1)
    own_weight = lax.dynamic_slice_in_dim(weight_sum, me * tok_dev, tok_dev, axis=1)
    total = jnp.sum(terms.astype(f32), axis=0)
    for e in range(n_seq):
        back = own_rank[e][:, None] == slot_ids[None, :]
        total = total + dot(back.astype(bf16), all_values[e]) * own_weight[e][:, None]
    own = lax.dynamic_slice_in_dim(merged, me * tok_dev, tok_dev, axis=0)
    return (own.astype(f32) + total).astype(bf16)[None]


def solution(mesh):
    placed = (
        P("fsdp", None, None),
        P("fsdp", None),
        P("fsdp", None),
        P("fsdp", "seq", None),
        P("fsdp", None, None),
        P("fsdp", None, None),
        P(),
        P("fsdp", "seq"),
        P("fsdp", "seq"),
        P(),
        P("fsdp", "seq"),
        P(),
        P("fsdp", "seq"),
        P("fsdp", "seq"),
        P("fsdp", "seq"),
        P("fsdp", "seq", None),
        P("fsdp", "seq", None),
        P("fsdp", "seq", None),
    )
    return jax.shard_map(
        shards, mesh=mesh, in_specs=placed, out_specs=P("fsdp", "seq", None), check_vma=False
    )
```

```python
import functools

import jax
import jax.numpy as jnp
from jax import lax
from jax.sharding import PartitionSpec as P

ln_epsilon = 1e-05
rms_epsilon = 1e-06
bf16 = jnp.bfloat16
f32 = jnp.float32


def layer_norm(values, gain_vec):
    center = values - jnp.mean(values, axis=-1, keepdims=True)
    spread = jnp.mean(center * center, axis=-1, keepdims=True)
    return center * lax.rsqrt(spread + ln_epsilon) * gain_vec


def rms_norm(values, gain_vec):
    square = jnp.mean(values * values, axis=-1, keepdims=True)
    return values * lax.rsqrt(square + rms_epsilon) * gain_vec


def visual_positions(counts, starts, total):
    images = jnp.arange(counts.shape[0], dtype=jnp.int32)
    end_index = jnp.sum(jnp.where(images[None, :] <= images[:, None], counts[None, :], 0), axis=1)
    begins = end_index - counts
    token_index = jnp.arange(total, dtype=jnp.int32)
    inside = (token_index[:, None] >= begins[None, :]) & (token_index[:, None] < end_index[None, :])
    placed = starts[None, :] + token_index[:, None] - begins[None, :]
    return jnp.sum(jnp.where(inside, placed, 0), axis=1)


def exchange(blocks, axis):
    return lax.all_to_all(blocks, axis, split_axis=0, concat_axis=0, tiled=True)


def spread_blocks(block, axis, count):
    return exchange(jnp.broadcast_to(block[None], (count,) + block.shape), axis)


def dot_t(left, right):
    return lax.dot_general(left, right, (((1,), (1,)), ((), ())), preferred_element_type=f32)


def dot(left, right):
    return jnp.dot(left, right, preferred_element_type=f32)


def shards(
    patches,
    counts,
    starts,
    embeds,
    route_ids,
    route_weights,
    vit_gain,
    vit_fc1,
    vit_fc2,
    proj_gain,
    proj_weight,
    moe_gain,
    shared_gate,
    shared_up,
    shared_down,
    expert_gate,
    expert_up,
    expert_down,
):
    n_seq = lax.axis_size("seq")
    me = lax.axis_index("seq")
    n_fsdp = lax.axis_size("fsdp")

    half = n_fsdp // 2
    swap = [(i, i ^ 1) for i in range(n_fsdp)]
    shifts = [[(i, (i + 2 * k) % n_fsdp) for i in range(n_fsdp)] for k in range(half)]

    width = embeds.shape[2]
    tok_dev = embeds.shape[1]
    all_embeds = spread_blocks(embeds[0], "seq", n_seq).reshape(n_seq * tok_dev, width)
    n_tok = n_seq * tok_dev

    vit_both = lax.all_gather(jnp.stack([vit_fc1, vit_fc2]), "fsdp", axis=1, tiled=True)
    proj_weight, vit_both, all_embeds = lax.optimization_barrier(
        (proj_weight, vit_both, all_embeds)
    )
    vit_first, vit_second = vit_both[0], vit_both[1]
    projector = lax.all_gather(proj_weight, "fsdp", axis=0, tiled=True)
    shared = jnp.stack([shared_gate, shared_up, shared_down])

    rows = patches.shape[1]
    my_rows = rows // n_seq
    normed = layer_norm(patches[0].astype(f32), vit_gain).astype(bf16)
    hidden = jax.nn.gelu(dot(normed, vit_first), approximate=True).astype(bf16)
    product = dot_t(hidden, vit_second).astype(bf16)
    blocks = exchange(product.reshape(n_seq, my_rows, product.shape[1]), "seq")
    shared, blocks = lax.optimization_barrier((shared, blocks))
    shared = lax.all_gather(shared, "fsdp", axis=1, tiled=True)
    gate_shared, up_shared, down_shared = shared[0], shared[1], shared[2]
    mixed = jnp.sum(blocks.astype(f32), axis=0)
    mine = lax.dynamic_slice_in_dim(patches[0], me * my_rows, my_rows, axis=0)
    residual = mine.astype(f32) + mixed

    joined = residual.shape[1] * 4
    proj_part = layer_norm(residual.reshape(-1, joined), proj_gain).astype(bf16)
    proj_in = spread_blocks(proj_part, "seq", n_seq).reshape(-1, joined)
    visual_part = dot(proj_in, projector).astype(bf16)
    n_vis = visual_part.shape[0]
    visual = spread_blocks(visual_part, "seq", n_seq).transpose(1, 0, 2).reshape(n_vis, width)

    positions = visual_positions(counts[0], starts[0], n_vis)
    token_ids = jnp.arange(n_tok, dtype=jnp.int32)
    place = positions[None, :] == token_ids[:, None]
    is_visual = jnp.any(place, axis=1)
    placed_visual = dot(place.astype(bf16), visual).astype(bf16)
    merged = jnp.where(is_visual[:, None], placed_visual, all_embeds)
    tokens = rms_norm(merged.astype(f32), moe_gain).astype(bf16)

    shared_hidden = (jax.nn.silu(dot(tokens, gate_shared)) * dot(tokens, up_shared)).astype(bf16)
    shared_value = dot_t(shared_hidden, down_shared).astype(bf16)

    capacity = n_tok // 8
    experts = jnp.arange(n_seq, dtype=jnp.int32)
    hit_mask = route_ids[0][None] == experts[:, None, None]
    chosen = jnp.any(hit_mask, axis=2)
    weight_sum = jnp.sum(jnp.where(hit_mask, route_weights[0][None], 0.0), axis=2)
    earlier = (token_ids[:, None] < token_ids[None, :]).astype(bf16)
    rank = dot(chosen.astype(bf16), earlier).astype(jnp.int32)
    rank = jnp.where(chosen, rank, -1)
    slot_ids = jnp.arange(capacity, dtype=jnp.int32)
    my_rank = lax.dynamic_index_in_dim(rank, me, 0, keepdims=False)
    pick = my_rank[None, :] == slot_ids[:, None]

    picked = dot(pick.astype(bf16), tokens).astype(bf16)
    depth = expert_gate.shape[0]
    hid = expert_gate.shape[2]
    core = lax.axis_index("fsdp") % 2
    picked_cols = exchange(picked.reshape(capacity, n_fsdp, depth).transpose(1, 0, 2), "fsdp")
    picked_cols = picked_cols.reshape(half, 2, capacity, depth).transpose(1, 0, 2, 3)
    picked_cols = picked_cols.reshape(n_fsdp * capacity, depth)
    gate_up = jnp.concatenate(
        [dot(picked_cols, expert_gate[:, 0, :]), dot(picked_cols, expert_up[:, 0, :])], axis=1
    ).astype(bf16)
    gate_up = gate_up.reshape(2, half * capacity, 2 * hid)
    keep = lax.dynamic_index_in_dim(gate_up, core, 0, keepdims=False)
    sent = lax.dynamic_index_in_dim(gate_up, 1 - core, 0, keepdims=False)
    sent = lax.ppermute(sent, "fsdp", swap)
    gate_up = (keep.astype(f32) + sent.astype(f32)).astype(bf16)
    gate_up = gate_up.reshape(half, capacity, 2 * hid)
    here = lax.axis_index("fsdp") // 2
    gate_up = jnp.concatenate([gate_up, gate_up], axis=0)
    gate_up = lax.dynamic_slice_in_dim(gate_up, here, half, axis=0)
    arrived = [gate_up[0]] + [lax.ppermute(gate_up[k], "fsdp", shifts[k]) for k in range(1, half)]
    shared_value, arrived = lax.optimization_barrier((shared_value, arrived))
    terms = exchange(shared_value.reshape(n_seq, tok_dev, width), "seq")
    sums = functools.reduce(jnp.add, [part.astype(f32) for part in arrived])
    expert_hidden = (jax.nn.silu(sums[:, :hid]) * sums[:, hid:]).astype(bf16)
    line_hidden = [expert_hidden]
    line_hidden += [lax.ppermute(expert_hidden, "fsdp", shifts[k]) for k in range(1, half)]
    other_hidden = [lax.ppermute(part, "fsdp", swap) for part in line_hidden]
    terms, other_hidden = lax.optimization_barrier((terms, other_hidden))
    weights = expert_down[:, 0, :]
    parts = [dot_t(part, weights).astype(bf16) for part in line_hidden[::-1] + other_hidden[::-1]]
    down_cols = jnp.stack(parts)
    down_cols = down_cols.reshape(2, half, capacity, depth)
    down_cols = jnp.concatenate([down_cols, down_cols], axis=1)
    down_cols = lax.dynamic_slice_in_dim(down_cols, half - 1 - here, half, axis=1)
    down_cols = jnp.concatenate([down_cols, down_cols], axis=0)
    down_cols = lax.dynamic_slice_in_dim(down_cols, core, 2, axis=0).transpose(1, 0, 2, 3)
    values = exchange(down_cols.reshape(n_fsdp, capacity, depth), "fsdp")
    values = values.transpose(1, 0, 2).reshape(capacity, width)
    my_weight = lax.dynamic_index_in_dim(weight_sum, me, 0, keepdims=False)
    slot_weight = jnp.sum(jnp.where(pick, my_weight[None, :], 0.0), axis=1)
    values = (values.astype(f32) * slot_weight[:, None]).astype(bf16)

    all_values = spread_blocks(values, "seq", n_seq)
    own_rank = lax.dynamic_slice_in_dim(rank, me * tok_dev, tok_dev, axis=1)
    back = own_rank.T[:, :, None] == slot_ids[None, None, :]
    back = back.astype(bf16).reshape(tok_dev, n_seq * capacity)
    total = jnp.sum(terms.astype(f32), axis=0)
    total = total + dot(back, all_values.reshape(n_seq * capacity, width))
    own = lax.dynamic_slice_in_dim(merged, me * tok_dev, tok_dev, axis=0)
    return (own.astype(f32) + total).astype(bf16)[None]


def solution(mesh):
    placed = (
        P("fsdp", None, None),
        P("fsdp", None),
        P("fsdp", None),
        P("fsdp", "seq", None),
        P("fsdp", None, None),
        P("fsdp", None, None),
        P(),
        P("fsdp", "seq"),
        P("fsdp", "seq"),
        P(),
        P("fsdp", "seq"),
        P(),
        P("fsdp", "seq"),
        P("fsdp", "seq"),
        P("fsdp", "seq"),
        P("fsdp", "seq", None),
        P("fsdp", "seq", None),
        P("fsdp", "seq", None),
    )
    return jax.shard_map(
        shards, mesh=mesh, in_specs=placed, out_specs=P("fsdp", "seq", None), check_vma=False
    )
```
